32 devices in a mesh: groups: 2 (over x), rows: 8 (over z, y), proj: 2 (over core).
Axes of the slice: x: 2, y: 2, z: 4, core: 2. Of those that a mesh axis runs over, the one named last changes fastest.
Arguments:
- train_rows: float32 [5120, 4, 8192], P(('groups', 'rows'), None, 'proj'), parts along dimension 0, may hold values from -6 to 6
- weights: float32 [5120, 4], P(('groups', 'rows', 'proj')), parts along dimension 0, may hold values from 0.1 to 1
- ckpt_index: int32 [320, 4], P(('groups', 'rows')), parts along dimension 0, may hold values from 0 to 3, each once within a row
- queries: float32 [512, 4, 8192], P(('groups', 'rows'), None, 'proj'), parts along dimension 0, may hold values from -0.125 to 0.125
Outputs:
- scores: float32 [5120, 256], P(('groups', 'rows'), 'proj'), parts along dimension 0
The draws below stay inside these ranges and needn't reach their ends.
There are 2 independent parts, one for each index of `groups`. The reference program is written for one: setup_inputs(seed, part) draws one part's arguments, and reference() takes and returns one part's arrays. A program takes and returns all parts, laid end to end along the dimension named above; each array names one. Nothing has to cross between parts.
Inputs may be any that keep to these rules, and one draw needn't show every extreme that they name: Each row of ckpt_index names every checkpoint once.
All inputs are finite; a program needn't handle non-finite values.
Results may differ from the reference program's by a relative error of at most 0.000073.
Values sent between devices are 32-bit elements; how exact they have to be, the bound alone decides.
A program may use at most 192 MiB of HBM per device.

```python
import math
import jax
import jax.numpy as jnp
from jax import lax

DIM = 8192
CKPTS = 4
ROWS = 2560
QUERIES = 256
SLABS = 160


def levels(key, shape, cuts, low, top_value):
    def one(dim, blocks):
        draws = jax.random.uniform(jax.random.fold_in(jax.random.fold_in(key, 6), dim), (blocks,), jnp.float32, low / len(cuts), top_value / len(cuts))
        return jnp.repeat(jnp.exp(draws), shape[dim] // blocks).reshape((-1,) + (1,) * (len(shape) - dim - 1))

    factor_of = one(*cuts[0])
    for cut in cuts[1:]:
        factor_of = factor_of * one(*cut)
    return factor_of


def noise(rng, dims, deviation, most, pieces=(), held_as=jnp.bfloat16):
    drawn = jax.random.normal(rng, dims, jnp.float32) * deviation
    if len(pieces) > 0:
        drawn = levels(rng, dims, pieces, -0.22, 0.18) * drawn
    return jnp.clip(drawn, min=-most, max=most).astype(held_as)


def setup_inputs(seed: int = 0, part: int = 0) -> dict:
    streams_of = jax.random.split(jax.random.key(seed), 5)
    own_keys = jax.random.split(jax.random.fold_in(streams_of[4], part), 5)
    train_rows = noise(own_keys[0], (ROWS, CKPTS, DIM), 1.0, 6.0, ((0, 8), (2, 2)), jnp.float32)
    weights = jnp.clip(jnp.exp(math.log(1.0) - 2.3025851 * jax.random.uniform(own_keys[1], (ROWS, CKPTS), jnp.float32) ** levels(own_keys[1], (ROWS, CKPTS), ((0, 16),), -0.2, 0.2)), 0.1, 1.0)
    ckpt_index = jax.vmap(lambda own: jax.random.permutation(own, CKPTS))(jax.random.split(own_keys[2], SLABS)).reshape((SLABS, CKPTS)).astype(jnp.int32)
    queries = noise(own_keys[3], (QUERIES, CKPTS, DIM), (DIM // 4) ** -0.5, 0.125, ((0, 8), (2, 2)), jnp.float32)
    return {"train_rows": train_rows, "weights": weights, "ckpt_index": ckpt_index, "queries": queries}


def reference(train_rows, weights, ckpt_index, queries):
    slab_rows = train_rows.shape[0] // ckpt_index.shape[0]
    slot_ckpt = jnp.repeat(ckpt_index, slab_rows, axis=0)
    onehot = (slot_ckpt[:, :, None] == jnp.arange(CKPTS, dtype=jnp.int32)[None, None, :]).astype(jnp.float32)
    weighted = weights[:, :, None] * train_rows
    by_ckpt = jnp.einsum("isc,isk->ick", onehot, weighted, precision=lax.Precision.HIGHEST)
    stacked = by_ckpt.reshape(ROWS, CKPTS * DIM)
    flat_queries = queries.reshape(QUERIES, CKPTS * DIM)
    scores = lax.dot_general(stacked, flat_queries, (((1,), (1,)), ((), ())), precision=lax.Precision.HIGHEST, preferred_element_type=jnp.float32)
    return scores * (1.0 / CKPTS)
```

```python
import functools

import jax
import jax.numpy as jnp
from jax import lax
from jax.experimental import pallas as pl
from jax.experimental.pallas import tpu as pltpu
from jax.sharding import PartitionSpec as P

MESH = pl.DeviceIdType.MESH
PIECES = 8
LAG = 2


def kernel(n, train, weights, ckpt, queries, gat, mine, theirs,
           th, tl, tbuf, qtile, acc, wfull, pout,
           recv, send, fetch, tsem, wsem, psem):
    line = n // 2
    main = PIECES - 1
    per_step = main + 2
    y_slots = PIECES + (line - 1) * main
    z_slots = (line - 1) * per_step
    slots = max(y_slots, z_slots)
    rows, ckpts, depth = train.shape
    count = queries.shape[0]
    width = depth // PIECES
    lanes = count * ckpts
    half_cols = mine.shape[1]

    me = lax.axis_index("rows")
    core = lax.axis_index("proj")
    z, y = lax.div(me, 2), lax.rem(me, 2)
    across = {"rows": z * 2 + (1 - y)}
    above = {"rows": me + 2}
    below = {"rows": me - 2}
    partner = {"proj": 1 - core}

    def part(ref, piece):
        return ref.at[:, :, pl.ds(pl.multiple_of(piece * width, width), width)]

    def by_arrival(k):
        m = jnp.minimum(z, line - 1 - z)
        far = k - m + 1
        near = jnp.where(lax.rem(k, 2) == 0, z - lax.div(k, 2) - 1, z + lax.div(k, 2) + 1)
        rest = jnp.where(2 * z < line - 1, z + far, z - far)
        return jnp.where(k < 2 * m, near, rest)

    def y_item(t, col):
        first = t < PIECES
        v = jnp.maximum(t - PIECES, 0)
        other = by_arrival(lax.div(v, main))
        zb = jnp.where(first, z, other)
        piece = jnp.where(first, lax.rem(t + PIECES - 1, PIECES), lax.rem(v, main))
        return zb * 2 + col, piece

    def z_item(t, start, sign):
        s, i = lax.div(t, per_step), lax.rem(t, per_step)
        zb = start + sign * s
        col = jnp.where(i == per_step - 1, 1 - y, y)
        piece = jnp.minimum(i, PIECES - 1)
        ok = (t < z_slots) & (zb >= 0) & (zb < line)
        own = (s == 0) & (i < PIECES)
        return jnp.clip(zb, 0, line - 1) * 2 + col, piece, ok, own

    def copy_to(src, block, piece, lane, u, device):
        return pltpu.make_async_remote_copy(
            src_ref=part(src, piece),
            dst_ref=part(gat.at[block], piece),
            send_sem=send.at[lane, lax.rem(u, 8)],
            recv_sem=recv.at[block, piece],
            device_id=device,
            device_id_type=MESH,
        )

    def sends(u):
        block, piece = y_item(u, y)

        @pl.when(u < PIECES)
        def _():
            copy_to(queries, block, piece, 0, u, across).start()

        @pl.when((u >= PIECES) & (u < y_slots))
        def _():
            copy_to(gat.at[block], block, piece, 0, u, across).start()

        for lane, device, sign, there in ((1, above, -1, z < line - 1), (2, below, 1, z > 0)):
            block, piece, ok, own = z_item(u, z, sign)

            @pl.when(there & ok & own)
            def _():
                copy_to(queries, block, piece, lane, u, device).start()

            @pl.when(there & ok & jnp.logical_not(own))
            def _():
                copy_to(gat.at[block], block, piece, lane, u, device).start()

    def wait_sends(u):
        @pl.when((u >= 0) & (u < y_slots))
        def _():
            copy_to(queries, me, 0, 0, u, across).wait_send()

        for lane, device, sign, there in ((1, above, -1, z < line - 1), (2, below, 1, z > 0)):
            ok = z_item(jnp.maximum(u, 0), z, sign)[2]

            @pl.when(there & ok & (u >= 0))
            def _():
                copy_to(queries, me, 0, lane, u, device).wait_send()

    def arrivals(t):
        block, piece = y_item(t, 1 - y)
        found = [(block, piece, t < y_slots)]
        for start, sign in ((z - 1, -1), (z + 1, 1)):
            block, piece, ok, _ = z_item(t, start, sign)
            found.append((block, piece, ok))
        found.append((me, lax.rem(t + PIECES - 1, PIECES), t < PIECES))
        return found

    def fetch_copy(src, piece, t, j):
        return pltpu.make_async_copy(part(src, piece), qtile.at[lax.rem(t, 2), j], fetch.at[lax.rem(t, 2), j])

    def take(t):
        for j, (block, piece, ok) in enumerate(arrivals(t)):
            @pl.when(ok)
            def _():
                if j < 3:
                    copy_to(queries, block, piece, 0, 0, across).wait_recv()
                    fetch_copy(gat.at[block], piece, t, j).start()
                else:
                    fetch_copy(queries, piece, t, j).start()

    def multiply(t):
        found = arrivals(t)

        def one(j, carry):
            def pick(values):
                return jnp.where(j == 0, values[0], jnp.where(j == 1, values[1], jnp.where(j == 2, values[2], values[3])))
            block = pick([f[0] for f in found])
            piece = pick([f[1] for f in found])
            ok = pick([f[2].astype(jnp.int32) for f in found])

            @pl.when(ok == 1)
            def _():
                fetch_copy(queries, 0, t, j).wait()
                q = qtile[lax.rem(t, 2), j].reshape(lanes, width)
                hi = q.astype(jnp.bfloat16)
                lo = (q - hi.astype(jnp.float32)).astype(jnp.bfloat16)
                ds = pl.ds(pl.multiple_of(piece * width, width), width)
                dims = (((1,), (1,)), ((), ()))
                both = jnp.concatenate([hi, lo], axis=0)
                r = lax.dot_general(th[:, ds], both, dims, preferred_element_type=jnp.float32)
                r2 = lax.dot_general(tl[:, ds], hi, dims, preferred_element_type=jnp.float32)
                acc[block] += r[:, :lanes] + r[:, lanes:] + r2
            return carry

        lax.fori_loop(0, 4, one, 0)

    def t_copy(u):
        return pltpu.make_async_copy(
            part(train, lax.rem(u + PIECES - 1, PIECES)), tbuf.at[lax.rem(u, 2)], tsem.at[lax.rem(u, 2)])

    def split(u):
        @pl.when(u + 1 < PIECES)
        def _():
            t_copy(u + 1).start()
        t_copy(u).wait()
        ds = pl.ds(pl.multiple_of(lax.rem(u + PIECES - 1, PIECES) * width, width), width)

        def some(r, carry):
            x = tbuf[lax.rem(u, 2), pl.ds(r * 16, 16)].reshape(16 * ckpts, width)
            hi = x.astype(jnp.bfloat16)
            out = pl.ds(pl.multiple_of(r * (16 * ckpts), 16 * ckpts), 16 * ckpts)
            th[out, ds] = hi
            tl[out, ds] = (x - hi.astype(jnp.float32)).astype(jnp.bfloat16)
            return carry

        lax.fori_loop(0, rows // 16, some, 0)

    t_copy(0).start()
    barrier = pltpu.get_barrier_semaphore()
    for device in (across, partner):
        pl.semaphore_signal(barrier, inc=1, device_id=device, device_id_type=MESH)

    @pl.when(z < line - 1)
    def _():
        pl.semaphore_signal(barrier, inc=1, device_id=above, device_id_type=MESH)

    @pl.when(z > 0)
    def _():
        pl.semaphore_signal(barrier, inc=1, device_id=below, device_id_type=MESH)

    pl.semaphore_wait(barrier, 2 + (z < line - 1).astype(jnp.int32) + (z > 0).astype(jnp.int32))

    here = weights.shape[0]
    w_copy = pltpu.make_async_remote_copy(
        src_ref=weights, dst_ref=wfull.at[core], send_sem=wsem.at[0], recv_sem=wsem.at[1],
        device_id=partner, device_id_type=MESH)

    def clear(b, carry):
        acc[b] = jnp.zeros(acc.shape[1:], jnp.float32)
        return carry

    def step(u, carry):
        @pl.when(u < slots)
        def _():
            sends(u)

        @pl.when(u == 0)
        def _():
            w_copy.start()
            wfull[core] = weights[...]
            lax.fori_loop(0, n, clear, 0)

        @pl.when((u >= LAG) & (u < slots + LAG))
        def _():
            take(u - LAG)

        @pl.when(u < PIECES)
        def _():
            split(u)

        @pl.when(u >= LAG + 1)
        def _():
            multiply(u - LAG - 1)

        wait_sends(u - 4)
        return carry

    last = slots + LAG + 1
    lax.fori_loop(0, last, step, 0)
    for u in range(last - 4, slots):
        wait_sends(u)
    w_copy.wait()

    w = jnp.concatenate([wfull[0], wfull[1]], axis=0)
    held = ckpt[...]
    of_lane = lax.broadcasted_iota(jnp.int32, (rows, lanes), 1) % ckpts
    coef = [jnp.where(held[:, s:s + 1] == of_lane, w[:, s:s + 1], 0.0) for s in range(ckpts)]

    def finish(half):
        def one(b, total):
            block = half * (n // 2) + b
            a = acc.at[block]
            mixed = coef[0] * a[pl.ds(0, rows, stride=ckpts), :]
            for s in range(1, ckpts):
                mixed += coef[s] * a[pl.ds(s, rows, stride=ckpts), :]
            lane = lax.broadcasted_iota(jnp.int32, (lanes, half_cols), 0)
            col = lax.broadcasted_iota(jnp.int32, (lanes, half_cols), 1)
            place = jnp.where(col - b * count == lane // ckpts, 1.0, 0.0).astype(jnp.float32)
            return total + lax.dot_general(mixed, place, (((1,), (0,)), ((), ())),
                                           precision=lax.Precision.HIGHEST,
                                           preferred_element_type=jnp.float32)
        return lax.fori_loop(0, n // 2, one, jnp.zeros((rows, half_cols), jnp.float32))

    pout[...] = finish(1 - core)
    back = pltpu.make_async_remote_copy(
        src_ref=pout, dst_ref=theirs, send_sem=psem.at[0], recv_sem=psem.at[1],
        device_id=partner, device_id_type=MESH)
    back.start()
    mine[...] = finish(core)
    back.wait()


def on_device(n, train_rows, weights, ckpt_index, queries):
    rows, ckpts, depth = train_rows.shape
    count = queries.shape[0]
    lanes = count * ckpts
    width = depth // PIECES
    half_cols = n * count // 2
    held = jnp.repeat(ckpt_index, rows // ckpt_index.shape[0], axis=0)
    anyspec = pl.BlockSpec(memory_space=pl.ANY)
    vmem = pl.BlockSpec(memory_space=pltpu.VMEM)
    part = jax.ShapeDtypeStruct((rows, half_cols), jnp.float32)
    _, mine, theirs = pl.pallas_call(
        functools.partial(kernel, n),
        out_shape=(jax.ShapeDtypeStruct((n,) + queries.shape, jnp.float32), part, part),
        in_specs=[anyspec, vmem, vmem, anyspec],
        out_specs=(anyspec, vmem, vmem),
        scratch_shapes=[
            pltpu.VMEM((rows * ckpts, depth), jnp.bfloat16),
            pltpu.VMEM((rows * ckpts, depth), jnp.bfloat16),
            pltpu.VMEM((2, rows, ckpts, width), jnp.float32),
            pltpu.VMEM((2, 4, count, ckpts, width), jnp.float32),
            pltpu.VMEM((n, rows * ckpts, lanes), jnp.float32),
            pltpu.VMEM((2, rows // 2, ckpts), jnp.float32),
            pltpu.VMEM((rows, half_cols), jnp.float32),
            pltpu.SemaphoreType.DMA((n, PIECES)),
            pltpu.SemaphoreType.DMA((3, 8)),
            pltpu.SemaphoreType.DMA((2, 4)),
            pltpu.SemaphoreType.DMA((2,)),
            pltpu.SemaphoreType.DMA((2,)),
            pltpu.SemaphoreType.DMA((2,)),
        ],
        compiler_params=pltpu.CompilerParams(
            collective_id=0, has_side_effects=True, vmem_limit_bytes=60 * 1024 * 1024),
        cost_estimate=pl.CostEstimate(
            flops=6 * rows * ckpts * depth * lanes * n, bytes_accessed=4 * rows * ckpts * depth, transcendentals=0),
    )(train_rows, weights, held, queries)
    return (mine + theirs) * (1.0 / ckpts)


def solution(mesh):
    placed = (
        P(("groups", "rows"), None, "proj"),
        P(("groups", "rows", "proj"), None),
        P(("groups", "rows"), None),
        P(("groups", "rows"), None, "proj"),
    )
    return jax.shard_map(
        functools.partial(on_device, mesh.shape["rows"]),
        mesh=mesh,
        in_specs=placed,
        out_specs=P(("groups", "rows"), "proj"),
        check_vma=False,
    )
```

```python
import functools

import jax
import jax.numpy as jnp
from jax import lax
from jax.experimental import pallas as pl
from jax.experimental.pallas import tpu as pltpu
from jax.sharding import PartitionSpec as P

MESH = pl.DeviceIdType.MESH
PIECES = 16
LAG = 3


def kernel(n, train, weights, ckpt, queries, gat, mine, theirs,
           th, tl, tbuf, qtile, acc, wfull, tot,
           recv, send, fetch, tsem, wsem, psem):
    line = n // 2
    early = max(1, (PIECES - LAG - 1) // (2 * max(1, line - 2)))
    main = PIECES - early
    per_step = PIECES + early
    y_slots = PIECES + (line - 1) * main
    z_slots = (line - 1) * per_step
    slots = max(y_slots, z_slots)
    rows, ckpts, depth = train.shape
    count = queries.shape[0]
    width = depth // PIECES
    lanes = count * ckpts
    half_cols = mine.shape[1]

    me = lax.axis_index("rows")
    core = lax.axis_index("proj")
    z, y = lax.div(me, 2), lax.rem(me, 2)
    across = {"rows": z * 2 + (1 - y)}
    above = {"rows": me + 2}
    below = {"rows": me - 2}
    partner = {"proj": 1 - core}

    def part(ref, piece):
        return ref.at[:, :, pl.ds(pl.multiple_of(piece * width, width), width)]

    def by_arrival(k):
        m = jnp.minimum(z, line - 1 - z)
        far = k - m + 1
        near = jnp.where(lax.rem(k, 2) == 0, z - lax.div(k, 2) - 1, z + lax.div(k, 2) + 1)
        rest = jnp.where(2 * z < line - 1, z + far, z - far)
        return jnp.where(k < 2 * m, near, rest)

    def y_item(t, col):
        first = t < PIECES
        v = jnp.maximum(t - PIECES, 0)
        other = by_arrival(lax.div(v, main))
        zb = jnp.where(first, z, other)
        piece = jnp.where(first, lax.rem(t + main, PIECES), lax.rem(v, main))
        return zb * 2 + col, piece

    def z_item(t, start, sign):
        s, i = lax.div(t, per_step), lax.rem(t, per_step)
        zb = start + sign * s
        col = jnp.where(i >= PIECES, 1 - y, y)
        piece = jnp.where(i >= PIECES, i - early, i)
        ok = (t < z_slots) & (zb >= 0) & (zb < line)
        own = (s == 0) & (i < PIECES)
        return jnp.clip(zb, 0, line - 1) * 2 + col, piece, ok, own

    def copy_to(src, block, piece, lane, u, device):
        return pltpu.make_async_remote_copy(
            src_ref=part(src, piece),
            dst_ref=part(gat.at[block], piece),
            send_sem=send.at[lane, lax.rem(u, 8)],
            recv_sem=recv.at[block, piece],
            device_id=device,
            device_id_type=MESH,
        )

    def sends(u):
        block, piece = y_item(u, y)

        @pl.when(u < PIECES)
        def _():
            copy_to(queries, block, piece, 0, u, across).start()

        @pl.when((u >= PIECES) & (u < y_slots))
        def _():
            copy_to(gat.at[block], block, piece, 0, u, across).start()

        for lane, device, sign, there in ((1, above, -1, z < line - 1), (2, below, 1, z > 0)):
            block, piece, ok, own = z_item(u, z, sign)

            @pl.when(there & ok & own)
            def _():
                copy_to(queries, block, piece, lane, u, device).start()

            @pl.when(there & ok & jnp.logical_not(own))
            def _():
                copy_to(gat.at[block], block, piece, lane, u, device).start()

    def wait_sends(u):
        @pl.when((u >= 0) & (u < y_slots))
        def _():
            copy_to(queries, me, 0, 0, u, across).wait_send()

        for lane, device, sign, there in ((1, above, -1, z < line - 1), (2, below, 1, z > 0)):
            ok = z_item(jnp.maximum(u, 0), z, sign)[2]

            @pl.when(there & ok & (u >= 0))
            def _():
                copy_to(queries, me, 0, lane, u, device).wait_send()

    def arrivals(t):
        block, piece = y_item(t, 1 - y)
        found = [(block, piece, t < y_slots)]
        for start, sign in ((z - 1, -1), (z + 1, 1)):
            block, piece, ok, _ = z_item(t, start, sign)
            found.append((block, piece, ok))
        found.append((me, lax.rem(t + main, PIECES), t < PIECES))
        return found

    def fetch_copy(src, piece, t, j):
        return pltpu.make_async_copy(part(src, piece), qtile.at[lax.rem(t, 2), j], fetch.at[lax.rem(t, 2), j])

    def take(t):
        for j, (block, piece, ok) in enumerate(arrivals(t)):
            @pl.when(ok)
            def _():
                if j < 3:
                    copy_to(queries, block, piece, 0, 0, across).wait_recv()
                    fetch_copy(gat.at[block], piece, t, j).start()
                else:
                    fetch_copy(queries, piece, t, j).start()

    def multiply(t):
        found = arrivals(t)

        def one(j, carry):
            def pick(values):
                return jnp.where(j == 0, values[0], jnp.where(j == 1, values[1], jnp.where(j == 2, values[2], values[3])))
            block = pick([f[0] for f in found])
            piece = pick([f[1] for f in found])
            ok = pick([f[2].astype(jnp.int32) for f in found])

            @pl.when(ok == 1)
            def _():
                fetch_copy(queries, 0, t, j).wait()
                q = qtile[lax.rem(t, 2), j].reshape(lanes, width)
                hi = q.astype(jnp.bfloat16)
                lo = (q - hi.astype(jnp.float32)).astype(jnp.bfloat16)
                ds = pl.ds(pl.multiple_of(piece * width, width), width)
                dims = (((1,), (1,)), ((), ()))
                both = jnp.concatenate([hi, lo], axis=0)
                r = lax.dot_general(th[:, ds], both, dims, preferred_element_type=jnp.float32)
                r2 = lax.dot_general(tl[:, ds], hi, dims, preferred_element_type=jnp.float32)
                acc[block] += r[:, :lanes] + r[:, lanes:] + r2
            return carry

        lax.fori_loop(0, 4, one, 0)

    def t_copy(u):
        return pltpu.make_async_copy(
            part(train, lax.rem(u + main, PIECES)), tbuf.at[lax.rem(u, 2)], tsem.at[lax.rem(u, 2)])

    def split(u):
        @pl.when(u + 1 < PIECES)
        def _():
            t_copy(u + 1).start()
        t_copy(u).wait()
        ds = pl.ds(pl.multiple_of(lax.rem(u + main, PIECES) * width, width), width)

        def some(r, carry):
            x = tbuf[lax.rem(u, 2), pl.ds(r * 16, 16)].reshape(16 * ckpts, width)
            hi = x.astype(jnp.bfloat16)
            out = pl.ds(pl.multiple_of(r * (16 * ckpts), 16 * ckpts), 16 * ckpts)
            th[out, ds] = hi
            tl[out, ds] = (x - hi.astype(jnp.float32)).astype(jnp.bfloat16)
            return carry

        lax.fori_loop(0, rows // 16, some, 0)

    t_copy(0).start()
    barrier = pltpu.get_barrier_semaphore()
    for device in (across, partner):
        pl.semaphore_signal(barrier, inc=1, device_id=device, device_id_type=MESH)

    @pl.when(z < line - 1)
    def _():
        pl.semaphore_signal(barrier, inc=1, device_id=above, device_id_type=MESH)

    @pl.when(z > 0)
    def _():
        pl.semaphore_signal(barrier, inc=1, device_id=below, device_id_type=MESH)

    pl.semaphore_wait(barrier, 2 + (z < line - 1).astype(jnp.int32) + (z > 0).astype(jnp.int32))

    here = weights.shape[0]
    w_copy = pltpu.make_async_remote_copy(
        src_ref=weights, dst_ref=wfull.at[core], send_sem=wsem.at[0], recv_sem=wsem.at[1],
        device_id=partner, device_id_type=MESH)

    def finish(zb):
        half = lax.div(zb, line // 2)
        first = (zb - half * (line // 2)) * 2 * count
        w = jnp.concatenate([wfull[0], wfull[1]], axis=0)
        held = ckpt[...]
        of_lane = lax.broadcasted_iota(jnp.int32, (rows, lanes), 1) % ckpts
        coef = [jnp.where(held[:, s:s + 1] == of_lane, w[:, s:s + 1], 0.0) for s in range(ckpts)]
        both = []
        for col in range(2):
            a = acc.at[zb * 2 + col]
            mixed = coef[0] * a[pl.ds(0, rows, stride=ckpts), :]
            for s in range(1, ckpts):
                mixed += coef[s] * a[pl.ds(s, rows, stride=ckpts), :]
            both.append(mixed)
        lane = lax.broadcasted_iota(jnp.int32, (2 * lanes, half_cols), 0)
        col = lax.broadcasted_iota(jnp.int32, (2 * lanes, half_cols), 1)
        place = jnp.where(col - first == lane // ckpts, 1.0, 0.0).astype(jnp.float32)
        tot[half] += lax.dot_general(
            jnp.concatenate(both, axis=1), place, (((1,), (0,)), ((), ())),
            precision=lax.Precision.HIGHEST, preferred_element_type=jnp.float32)

    full_from = max(PIECES + main * (line - 2), per_step * (line - 2)) + LAG + 1

    def clear(b, carry):
        acc[b] = jnp.zeros(acc.shape[1:], jnp.float32)
        return carry

    def step(u, carry):
        @pl.when(u < slots)
        def _():
            sends(u)

        @pl.when(u == 0)
        def _():
            w_copy.start()
            wfull[core] = weights[...]
            lax.fori_loop(0, n, clear, 0)
            tot[...] = jnp.zeros(tot.shape, jnp.float32)

        @pl.when((u >= LAG) & (u < slots + LAG))
        def _():
            take(u - LAG)

        @pl.when(u < PIECES)
        def _():
            split(u)

        @pl.when(u >= LAG + 1)
        def _():
            multiply(u - LAG - 1)

        e = u - full_from

        @pl.when(e == 0)
        def _():
            w_copy.wait()

        @pl.when((e >= 0) & (e < line - 1))
        def _():
            finish(jnp.where(e == 0, z, by_arrival(jnp.maximum(e - 1, 0))))

        wait_sends(u - 5)
        return carry

    last = slots + LAG + 1
    lax.fori_loop(0, last, step, 0)
    for u in range(last - 5, slots):
        wait_sends(u)
    finish(by_arrival(line - 2))

    back = pltpu.make_async_remote_copy(
        src_ref=tot.at[1 - core], dst_ref=theirs, send_sem=psem.at[0], recv_sem=psem.at[1],
        device_id=partner, device_id_type=MESH)
    back.start()
    mine[...] = tot[core]
    back.wait()


def on_device(n, train_rows, weights, ckpt_index, queries):
    rows, ckpts, depth = train_rows.shape
    count = queries.shape[0]
    lanes = count * ckpts
    width = depth // PIECES
    half_cols = n * count // 2
    held = jnp.repeat(ckpt_index, rows // ckpt_index.shape[0], axis=0)
    anyspec = pl.BlockSpec(memory_space=pl.ANY)
    vmem = pl.BlockSpec(memory_space=pltpu.VMEM)
    part = jax.ShapeDtypeStruct((rows, half_cols), jnp.float32)
    _, mine, theirs = pl.pallas_call(
        functools.partial(kernel, n),
        out_shape=(jax.ShapeDtypeStruct((n,) + queries.shape, jnp.float32), part, part),
        in_specs=[anyspec, vmem, vmem, anyspec],
        out_specs=(anyspec, vmem, vmem),
        scratch_shapes=[
            pltpu.VMEM((rows * ckpts, depth), jnp.bfloat16),
            pltpu.VMEM((rows * ckpts, depth), jnp.bfloat16),
            pltpu.VMEM((2, rows, ckpts, width), jnp.float32),
            pltpu.VMEM((2, 4, count, ckpts, width), jnp.float32),
            pltpu.VMEM((n, rows * ckpts, lanes), jnp.float32),
            pltpu.VMEM((2, rows // 2, ckpts), jnp.float32),
            pltpu.VMEM((2, rows, half_cols), jnp.float32),
            pltpu.SemaphoreType.DMA((n, PIECES)),
            pltpu.SemaphoreType.DMA((3, 8)),
            pltpu.SemaphoreType.DMA((2, 4)),
            pltpu.SemaphoreType.DMA((2,)),
            pltpu.SemaphoreType.DMA((2,)),
            pltpu.SemaphoreType.DMA((2,)),
        ],
        compiler_params=pltpu.CompilerParams(
            collective_id=0, has_side_effects=True, vmem_limit_bytes=60 * 1024 * 1024),
        cost_estimate=pl.CostEstimate(
            flops=6 * rows * ckpts * depth * lanes * n, bytes_accessed=4 * rows * ckpts * depth, transcendentals=0),
    )(train_rows, weights, held, queries)
    return (mine + theirs) * (1.0 / ckpts)


def solution(mesh):
    placed = (
        P(("groups", "rows"), None, "proj"),
        P(("groups", "rows", "proj"), None),
        P(("groups", "rows"), None),
        P(("groups", "rows"), None, "proj"),
    )
    return jax.shard_map(
        functools.partial(on_device, mesh.shape["rows"]),
        mesh=mesh,
        in_specs=placed,
        out_specs=P(("groups", "rows"), "proj"),
        check_vma=False,
    )
```

```python
import functools

import jax
import jax.numpy as jnp
from jax import lax
from jax.experimental import pallas as pl
from jax.experimental.pallas import tpu as pltpu
from jax.sharding import PartitionSpec as P

MESH = pl.DeviceIdType.MESH
PIECES = 16
LAG = 3


def kernel(n, train, weights, ckpt, queries, gat, mine, theirs,
           th, tl, tbuf, qtile, acc, wfull, wcol, hcol, tot,
           recv, send, fetch, tsem, wsem, psem):
    line = n // 2
    early = max(1, (PIECES - LAG - 1) // (2 * max(1, line - 2)))
    main = PIECES - early
    per_step = PIECES + early
    y_slots = PIECES + (line - 1) * main
    z_slots = (line - 1) * per_step
    slots = max(y_slots, z_slots)
    rows, ckpts, depth = train.shape
    count = queries.shape[0]
    width = depth // PIECES
    lanes = count * ckpts
    half_cols = mine.shape[1]

    me = lax.axis_index("rows")
    core = lax.axis_index("proj")
    z, y = lax.div(me, 2), lax.rem(me, 2)
    across = {"rows": z * 2 + (1 - y)}
    above = {"rows": me + 2}
    below = {"rows": me - 2}
    partner = {"proj": 1 - core}

    def part(ref, piece):
        return ref.at[:, :, pl.ds(pl.multiple_of(piece * width, width), width)]

    def by_arrival(k):
        m = jnp.minimum(z, line - 1 - z)
        far = k - m + 1
        near = jnp.where(lax.rem(k, 2) == 0, z - lax.div(k, 2) - 1, z + lax.div(k, 2) + 1)
        rest = jnp.where(2 * z < line - 1, z + far, z - far)
        return jnp.where(k < 2 * m, near, rest)

    def y_item(t, col):
        first = t < PIECES
        v = jnp.maximum(t - PIECES, 0)
        other = by_arrival(lax.div(v, main))
        zb = jnp.where(first, z, other)
        piece = jnp.where(first, lax.rem(t + main, PIECES), lax.rem(v, main))
        return zb * 2 + col, piece

    def z_item(t, start, sign):
        s, i = lax.div(t, per_step), lax.rem(t, per_step)
        zb = start + sign * s
        col = jnp.where(i >= PIECES, 1 - y, y)
        piece = jnp.where(i >= PIECES, i - early, i)
        ok = (t < z_slots) & (zb >= 0) & (zb < line)
        own = (s == 0) & (i < PIECES)
        return jnp.clip(zb, 0, line - 1) * 2 + col, piece, ok, own

    def copy_to(src, block, piece, lane, u, device):
        return pltpu.make_async_remote_copy(
            src_ref=part(src, piece),
            dst_ref=part(gat.at[block], piece),
            send_sem=send.at[lane, lax.rem(u, 8)],
            recv_sem=recv.at[block, piece],
            device_id=device,
            device_id_type=MESH,
        )

    def sends(u):
        block, piece = y_item(u, y)

        @pl.when(u < PIECES)
        def _():
            copy_to(queries, block, piece, 0, u, across).start()

        @pl.when((u >= PIECES) & (u < y_slots))
        def _():
            copy_to(gat.at[block], block, piece, 0, u, across).start()

        for lane, device, sign, there in ((1, above, -1, z < line - 1), (2, below, 1, z > 0)):
            block, piece, ok, own = z_item(u, z, sign)

            @pl.when(there & ok & own)
            def _():
                copy_to(queries, block, piece, lane, u, device).start()

            @pl.when(there & ok & jnp.logical_not(own))
            def _():
                copy_to(gat.at[block], block, piece, lane, u, device).start()

    def wait_sends(u):
        @pl.when((u >= 0) & (u < y_slots))
        def _():
            copy_to(queries, me, 0, 0, u, across).wait_send()

        for lane, device, sign, there in ((1, above, -1, z < line - 1), (2, below, 1, z > 0)):
            ok = z_item(jnp.maximum(u, 0), z, sign)[2]

            @pl.when(there & ok & (u >= 0))
            def _():
                copy_to(queries, me, 0, lane, u, device).wait_send()

    def arrivals(t):
        block, piece = y_item(t, 1 - y)
        found = [(block, piece, t < y_slots)]
        for start, sign in ((z - 1, -1), (z + 1, 1)):
            block, piece, ok, _ = z_item(t, start, sign)
            found.append((block, piece, ok))
        found.append((me, lax.rem(t + main, PIECES), t < PIECES))
        return found

    def fetch_copy(src, piece, t, j):
        return pltpu.make_async_copy(part(src, piece), qtile.at[lax.rem(t, 2), j], fetch.at[lax.rem(t, 2), j])

    def take(t):
        for j, (block, piece, ok) in enumerate(arrivals(t)):
            @pl.when(ok)
            def _():
                if j < 3:
                    copy_to(queries, block, piece, 0, 0, across).wait_recv()
                    fetch_copy(gat.at[block], piece, t, j).start()
                else:
                    fetch_copy(queries, piece, t, j).start()

    def multiply(t):
        found = arrivals(t)

        def one(j, carry):
            def pick(values):
                return jnp.where(j == 0, values[0], jnp.where(j == 1, values[1], jnp.where(j == 2, values[2], values[3])))
            block = pick([f[0] for f in found])
            piece = pick([f[1] for f in found])
            ok = pick([f[2].astype(jnp.int32) for f in found])

            @pl.when(ok == 1)
            def _():
                fetch_copy(queries, 0, t, j).wait()
                q = qtile[lax.rem(t, 2), j].reshape(lanes, width)
                hi = q.astype(jnp.bfloat16)
                lo = (q - hi.astype(jnp.float32)).astype(jnp.bfloat16)
                ds = pl.ds(pl.multiple_of(piece * width, width), width)
                dims = (((1,), (1,)), ((), ()))
                both = jnp.concatenate([hi, lo], axis=0)
                r = lax.dot_general(th[:, ds], both, dims, preferred_element_type=jnp.float32)
                r2 = lax.dot_general(tl[:, ds], hi, dims, preferred_element_type=jnp.float32)
                acc[block] += r[:, :lanes] + r[:, lanes:] + r2
            return carry

        lax.fori_loop(0, 4, one, 0)

    def t_copy(u):
        return pltpu.make_async_copy(
            part(train, lax.rem(u + main, PIECES)), tbuf.at[lax.rem(u, 2)], tsem.at[lax.rem(u, 2)])

    def split(u):
        @pl.when(u + 1 < PIECES)
        def _():
            t_copy(u + 1).start()
        t_copy(u).wait()
        ds = pl.ds(pl.multiple_of(lax.rem(u + main, PIECES) * width, width), width)

        def some(r, carry):
            x = tbuf[lax.rem(u, 2), pl.ds(r * 16, 16)].reshape(16 * ckpts, width)
            hi = x.astype(jnp.bfloat16)
            out = pl.ds(pl.multiple_of(r * (16 * ckpts), 16 * ckpts), 16 * ckpts)
            th[out, ds] = hi
            tl[out, ds] = (x - hi.astype(jnp.float32)).astype(jnp.bfloat16)
            return carry

        lax.fori_loop(0, rows // 16, some, 0)

    t_copy(0).start()
    barrier = pltpu.get_barrier_semaphore()
    for device in (across, partner):
        pl.semaphore_signal(barrier, inc=1, device_id=device, device_id_type=MESH)

    @pl.when(z < line - 1)
    def _():
        pl.semaphore_signal(barrier, inc=1, device_id=above, device_id_type=MESH)

    @pl.when(z > 0)
    def _():
        pl.semaphore_signal(barrier, inc=1, device_id=below, device_id_type=MESH)

    pl.semaphore_wait(barrier, 2 + (z < line - 1).astype(jnp.int32) + (z > 0).astype(jnp.int32))

    w_copy = pltpu.make_async_remote_copy(
        src_ref=weights, dst_ref=wfull.at[core], send_sem=wsem.at[0], recv_sem=wsem.at[1],
        device_id=partner, device_id_type=MESH)

    def finish(zb):
        half = lax.div(zb, line // 2)
        first = (zb - half * (line // 2)) * 2 * count
        w, held = wcol[...], hcol[...]
        of_lane = (lax.broadcasted_iota(jnp.int32, (rows, lanes), 1) % ckpts).astype(jnp.float32)
        coef = [jnp.where(held[:, s:s + 1] == of_lane, w[:, s:s + 1], 0.0) for s in range(ckpts)]
        both = []
        for col in range(2):
            a = acc.at[zb * 2 + col]
            mixed = coef[0] * a[pl.ds(0, rows, stride=ckpts), :]
            for s in range(1, ckpts):
                mixed += coef[s] * a[pl.ds(s, rows, stride=ckpts), :]
            both.append(mixed)
        lane = lax.broadcasted_iota(jnp.int32, (2 * lanes, half_cols), 0)
        col = lax.broadcasted_iota(jnp.int32, (2 * lanes, half_cols), 1)
        place = jnp.where(col - first == lane // ckpts, 1.0, 0.0).astype(jnp.float32)
        tot[half] += lax.dot_general(
            jnp.concatenate(both, axis=1), place, (((1,), (0,)), ((), ())),
            precision=lax.Precision.HIGHEST, preferred_element_type=jnp.float32)

    full_from = max(PIECES + main * (line - 2), per_step * (line - 2)) + LAG + 1

    def clear(b, carry):
        acc[b] = jnp.zeros(acc.shape[1:], jnp.float32)
        return carry

    def step(u, carry):
        @pl.when(u < slots)
        def _():
            sends(u)

        @pl.when(u == 0)
        def _():
            w_copy.start()
            wfull[core] = weights[...]
            lax.fori_loop(0, n, clear, 0)
            tot[...] = jnp.zeros(tot.shape, jnp.float32)

        @pl.when((u >= LAG) & (u < slots + LAG))
        def _():
            take(u - LAG)

        @pl.when(u < PIECES)
        def _():
            split(u)

        @pl.when(u >= LAG + 1)
        def _():
            multiply(u - LAG - 1)

        e = u - full_from

        @pl.when(e == 0)
        def _():
            w_copy.wait()
            for c in range(2):
                wcol[pl.ds(c * (rows // 2), rows // 2)] = wfull[c].T
            slabs = ckpt.shape[1]
            slab = lax.broadcasted_iota(jnp.int32, (slabs, rows), 0)
            row = lax.broadcasted_iota(jnp.int32, (slabs, rows), 1)
            spread = jnp.where(row // (rows // slabs) == slab, 1.0, 0.0).astype(jnp.float32)
            hcol[...] = jnp.dot(ckpt[...].astype(jnp.float32), spread, preferred_element_type=jnp.float32).T

        @pl.when((e >= 0) & (e < line - 1))
        def _():
            finish(jnp.where(e == 0, z, by_arrival(jnp.maximum(e - 1, 0))))

        wait_sends(u - 5)
        return carry

    last = slots + LAG + 1
    lax.fori_loop(0, last, step, 0)
    for u in range(last - 5, slots):
        wait_sends(u)
    finish(by_arrival(line - 2))

    back = pltpu.make_async_remote_copy(
        src_ref=tot.at[1 - core], dst_ref=theirs, send_sem=psem.at[0], recv_sem=psem.at[1],
        device_id=partner, device_id_type=MESH)
    back.start()
    mine[...] = tot[core]
    back.wait()


def on_device(n, train_rows, weights, ckpt_index, queries):
    rows, ckpts, depth = train_rows.shape
    count = queries.shape[0]
    lanes = count * ckpts
    width = depth // PIECES
    half_cols = n * count // 2
    anyspec = pl.BlockSpec(memory_space=pl.ANY)
    vmem = pl.BlockSpec(memory_space=pltpu.VMEM)
    part = jax.ShapeDtypeStruct((rows, half_cols), jnp.float32)
    _, mine, theirs = pl.pallas_call(
        functools.partial(kernel, n),
        out_shape=(jax.ShapeDtypeStruct((n,) + queries.shape, jnp.float32), part, part),
        in_specs=[anyspec, vmem, vmem, anyspec],
        out_specs=(anyspec, vmem, vmem),
        scratch_shapes=[
            pltpu.VMEM((rows * ckpts, depth), jnp.bfloat16),
            pltpu.VMEM((rows * ckpts, depth), jnp.bfloat16),
            pltpu.VMEM((2, rows, ckpts, width), jnp.float32),
            pltpu.VMEM((2, 4, count, ckpts, width), jnp.float32),
            pltpu.VMEM((n, rows * ckpts, lanes), jnp.float32),
            pltpu.VMEM((2, ckpts, rows // 2), jnp.float32),
            pltpu.VMEM((rows, ckpts), jnp.float32),
            pltpu.VMEM((rows, ckpts), jnp.float32),
            pltpu.VMEM((2, rows, half_cols), jnp.float32),
            pltpu.SemaphoreType.DMA((n, PIECES)),
            pltpu.SemaphoreType.DMA((3, 8)),
            pltpu.SemaphoreType.DMA((2, 4)),
            pltpu.SemaphoreType.DMA((2,)),
            pltpu.SemaphoreType.DMA((2,)),
            pltpu.SemaphoreType.DMA((2,)),
        ],
        compiler_params=pltpu.CompilerParams(
            collective_id=0, has_side_effects=True, vmem_limit_bytes=60 * 1024 * 1024),
        cost_estimate=pl.CostEstimate(
            flops=6 * rows * ckpts * depth * lanes * n, bytes_accessed=4 * rows * ckpts * depth, transcendentals=0),
    )(train_rows, weights.T, ckpt_index.T, queries)
    return (mine + theirs) * (1.0 / ckpts)


def solution(mesh):
    placed = (
        P(("groups", "rows"), None, "proj"),
        P(("groups", "rows", "proj"), None),
        P(("groups", "rows"), None),
        P(("groups", "rows"), None, "proj"),
    )
    return jax.shard_map(
        functools.partial(on_device, mesh.shape["rows"]),
        mesh=mesh,
        in_specs=placed,
        out_specs=P(("groups", "rows"), "proj"),
        check_vma=False,
    )
```
